256 devices in a mesh: row: 16 (over z_hi, y, core), col: 16 (over x, z_lo).
Axes of the slice: x: 4, y: 4, z: 8 (z_hi: 2, z_lo: 4; z = z_hi * 4 + z_lo), core: 2. Of those that a mesh axis runs over, the one named last changes fastest.
Arguments:
- amplitudes: bfloat16 [1024, 640, 640], P('col', None, 'row'), may hold values from -6 to 6
- integrals: bfloat16 [1536, 640, 640], P('col', 'row'), may hold values from -0.009765625 to 0.009765625
- owners: int32 [2], replicated, may hold values from 0 to 15
- offsets: int32 [2], replicated, may hold values from 0 to 32
Outputs:
- ladder_residual: float32 [1024, 128], P(('col', 'row'))
The draws below stay inside these ranges and needn't reach their ends.
All inputs are finite; a program needn't handle non-finite values.
Results may differ from the reference program's by a relative error of at most 0.0003.
Values may be sent and summed in bfloat16 or wider, within the bound.
No kernel may reach another device: no remote copies, remote signals or barrier semaphores. Data moves between devices by JAX's collectives and lax.ppermute only.
A program may use at most 128 MiB of HBM per device.

```python
import jax
import jax.numpy as jnp
from jax import lax

NV = 640
PR = 64
AB_LOC = 96
STEPS = 2
NIJ = 1024
AB = 1536
N_COL = 16


def levels(stream_key, shape, pieces, low, top_value):
    def one(axis_at, blocks):
        steps = jax.random.uniform(jax.random.fold_in(jax.random.fold_in(stream_key, 6), axis_at), (blocks,), jnp.float32, low / len(pieces), top_value / len(pieces))
        return jnp.repeat(jnp.exp(steps), shape[axis_at] // blocks).reshape((-1,) + (1,) * (len(shape) - axis_at - 1))

    loudness = one(*pieces[0])
    for cut in pieces[1:]:
        loudness = loudness * one(*cut)
    return loudness


def centred(key, shape, width, limit, shards=(), dtype=jnp.bfloat16):
    result = jax.random.normal(key, shape, jnp.float32) * width
    if len(shards) > 0:
        result = levels(key, shape, shards, -0.22, 0.18) * result
    return jnp.clip(result, min=-limit, max=limit).astype(dtype)


def setup_inputs(seed: int = 0) -> dict:
    key_list = jax.random.split(jax.random.key(seed), 5)
    amplitudes = centred(key_list[0], (NIJ, NV, NV), 1.0, 6.0, ((0, 16), (2, 16)))
    integrals = centred(key_list[1], (AB, NV, NV), (NV * NV) ** -0.5, 0.009765625, ((0, 16), (1, 16)))
    owners = jax.random.randint(key_list[2], (STEPS,), 0, N_COL).astype(jnp.int32)
    offsets = jax.random.randint(key_list[3], (STEPS,), 0, AB_LOC - PR + 1).astype(jnp.int32)
    return {"amplitudes": amplitudes, "integrals": integrals, "owners": owners, "offsets": offsets}


def reference(amplitudes, integrals, owners, offsets):
    flat = amplitudes.reshape(NIJ, NV * NV)
    blocks = []
    for step in range(STEPS):
        start = (owners[step] * AB_LOC + offsets[step]).astype(jnp.int32)
        panel = lax.dynamic_slice_in_dim(integrals, start, PR, 0).reshape(PR, NV * NV)
        blocks.append(lax.dot_general(flat, panel, (((1,), (1,)), ((), ())), preferred_element_type=jnp.float32))
    return jnp.concatenate(blocks, axis=1)
```

```python
import functools

import jax
import jax.numpy as jnp
from jax import lax
from jax.experimental import pallas as pl
from jax.experimental.pallas import tpu as pltpu
from jax.sharding import PartitionSpec as P

PR = 64
STEPS = 2
X = 4
ZL = 4
COL = 16
ROW = 16
BLOCK = 40
HALF = 20
PAIRS = 64
LANES = 128


def turned(ref):
    stacked = jnp.concatenate([ref[0, 0], ref[1, 0]], axis=0)
    return stacked.T.reshape(16, BLOCK, LANES)


def panel_kernel(in_ref, *out_refs):
    tiles = turned(in_ref)
    for row in range(ROW):
        out_refs[row][0] = tiles[row]


def amplitude_kernel(place_ref, in_ref, *refs):
    out_refs, held = refs[:X], refs[X]
    held[...] = turned(in_ref)
    x, zl = place_ref[0], place_ref[1]
    for kx in range(X):
        for kz in range(ZL):
            block = lax.rem(x + kx, X) * ZL + lax.rem(zl + kz, ZL)
            out_refs[kx][kz, 0] = held[block]


def turn_panel(swapped):
    piece = jax.ShapeDtypeStruct((HALF, BLOCK, LANES), jnp.bfloat16)
    return pl.pallas_call(
        panel_kernel,
        grid=(HALF,),
        in_specs=[pl.BlockSpec((2, 1, 64, 640), lambda i: (0, i, 0, 0))],
        out_specs=[pl.BlockSpec((1, BLOCK, LANES), lambda i: (i, 0, 0))] * ROW,
        out_shape=[piece] * ROW,
        compiler_params=pltpu.CompilerParams(vmem_limit_bytes=24 * 2**20),
        cost_estimate=pl.CostEstimate(flops=0, bytes_accessed=2 * 64 * 25600 * 2, transcendentals=0),
    )(swapped.reshape(2, HALF, 64, 640))


def turn_amplitudes(swapped, place):
    piece = jax.ShapeDtypeStruct((ZL, HALF, BLOCK, LANES), jnp.bfloat16)
    return pl.pallas_call(
        amplitude_kernel,
        grid_spec=pltpu.PrefetchScalarGridSpec(
            num_scalar_prefetch=1,
            grid=(HALF,),
            in_specs=[pl.BlockSpec((2, 1, 64, 640), lambda i, place: (0, i, 0, 0))],
            out_specs=[pl.BlockSpec((ZL, 1, BLOCK, LANES), lambda i, place: (0, i, 0, 0))] * X,
            scratch_shapes=[pltpu.VMEM((16, BLOCK, LANES), jnp.bfloat16)],
        ),
        out_shape=[piece] * X,
        compiler_params=pltpu.CompilerParams(vmem_limit_bytes=24 * 2**20),
        cost_estimate=pl.CostEstimate(flops=0, bytes_accessed=2 * 64 * 25600 * 2, transcendentals=0),
    )(place, swapped.reshape(2, HALF, 64, 640))


def contract_kernel(*refs):
    left, right, out_ref = refs[:X], refs[X : X + ZL], refs[X + ZL]
    for kx in range(X):
        total = jnp.zeros((LANES, 2 * LANES), jnp.float32)
        for kz in range(ZL):
            total += lax.dot_general(
                left[kx][kz], right[kz][...], (((0,), (0,)), ((), ())), preferred_element_type=jnp.float32
            )
        out_ref[kx] = total[:PAIRS, :LANES] + total[PAIRS:, LANES:]


def contract(left, right):
    depth = HALF * BLOCK
    left = [part.reshape(ZL, depth, LANES) for part in left]
    right = [part.reshape(depth, 2 * LANES) for part in right]
    return pl.pallas_call(
        contract_kernel,
        in_specs=[pl.BlockSpec(memory_space=pltpu.VMEM)] * (X + ZL),
        out_specs=pl.BlockSpec(memory_space=pltpu.VMEM),
        out_shape=jax.ShapeDtypeStruct((X, PAIRS, LANES), jnp.float32),
        compiler_params=pltpu.CompilerParams(vmem_limit_bytes=32 * 2**20),
        cost_estimate=pl.CostEstimate(flops=2 * 512 * 3200 * 256, bytes_accessed=5 * 2**20, transcendentals=0),
    )(*left, *right)


def shift_x(array, k):
    return lax.ppermute(array, "col", [(x * ZL + z, (x + k) % X * ZL + z) for x in range(X) for z in range(ZL)])


def shift_zl(array, k):
    return lax.ppermute(array, "col", [(x * ZL + z, x * ZL + (z - k) % ZL) for x in range(X) for z in range(ZL)])


def scatter_from(owner, *pieces):
    total = None
    for row in range(ROW):
        pairs = [(source * COL + owner, row * COL + source) for source in range(ROW)]
        got = lax.ppermute(pieces[row], ("row", "col"), pairs)
        total = got if total is None else total + got
    return total


def scatter(owner, pieces):
    return lax.switch(owner, [functools.partial(scatter_from, o) for o in range(COL)], *pieces)


def local(amplitudes, integrals, owners, offsets):
    col = lax.axis_index("col")
    place = jnp.stack([col // ZL, col % ZL]).astype(jnp.int32)
    pieces = []
    for step in range(STEPS):
        panel = lax.dynamic_slice_in_dim(integrals, offsets[step], PR, 0)
        pieces.append(turn_panel(jnp.transpose(panel, (1, 0, 2))))
    left = turn_amplitudes(jnp.transpose(amplitudes, (2, 0, 1)), place)
    left = [left[0]] + [shift_x(left[k], k) for k in range(1, X)]
    got = jnp.stack([scatter(owners[step], pieces[step]) for step in range(STEPS)])
    got = got.reshape(STEPS, HALF, 2, HALF, 2, PR)
    mine = jnp.transpose(got, (3, 4, 1, 2, 0, 5)).reshape(HALF, BLOCK, 2 * LANES)
    right = [mine] + [shift_zl(mine, k) for k in range(1, ZL)]
    part = contract(left, right)
    total = part[0]
    for k in range(1, X):
        total = total + shift_x(part[k], -k)
    spread = lax.all_to_all(total.reshape(ROW, PAIRS // ROW, LANES), "row", 0, 0, tiled=True)
    return jnp.sum(spread, axis=0)


def solution(mesh):
    in_specs = (P("col", None, "row"), P("col", "row", None), P(), P())
    out_specs = P(("col", "row"), None)
    return jax.shard_map(local, mesh=mesh, in_specs=in_specs, out_specs=out_specs, check_vma=False)
```

```python
import functools

import jax
import jax.numpy as jnp
from jax import lax
from jax.experimental import pallas as pl
from jax.experimental.pallas import tpu as pltpu
from jax.sharding import Mesh
from jax.sharding import PartitionSpec as P

PR = 64
STEPS = 2
X = 4
ZL = 4
ROW = ("zh", "y", "core")
COL = ("x", "zl")
ROWS = 16
NV = 640
BLOCK = 40
PIECE = 10
PAIRS = 64
LANES = 128
QUARTER = NV // X
DEPTH = PIECE * QUARTER


def panel_kernel(source_ref, in_ref, out_ref):
    out_ref[0, 0] = in_ref[0, 0].T


def turn_panel(pieces, sources):
    count, halves = sources.shape[0], PIECE // 2
    return pl.pallas_call(
        panel_kernel,
        grid_spec=pltpu.PrefetchScalarGridSpec(
            num_scalar_prefetch=1,
            grid=(count, halves),
            in_specs=[pl.BlockSpec((1, 1, LANES, NV), lambda p, i, source: (source[p], i, 0, 0))],
            out_specs=pl.BlockSpec((1, 1, NV, LANES), lambda p, i, source: (p, i, 0, 0)),
        ),
        out_shape=jax.ShapeDtypeStruct((count, halves, NV, LANES), jnp.bfloat16),
        compiler_params=pltpu.CompilerParams(vmem_limit_bytes=16 * 2**20),
        cost_estimate=pl.CostEstimate(flops=0, bytes_accessed=count * 2 * LANES * NV * PIECE, transcendentals=0),
    )(sources, pieces)


def amplitude_kernel(place_ref, first_ref, second_ref, *refs):
    out_refs, held = refs[:X], refs[X]
    stacked = jnp.concatenate([first_ref[0], second_ref[0]], axis=0)
    held[...] = stacked.T.astype(jnp.float32)
    for k in range(X):
        quarter = lax.rem(place_ref[0] + k, X)
        out_refs[k][0] = held[pl.ds(quarter, QUARTER, stride=X), :].astype(jnp.bfloat16)


def turn_amplitudes(swapped, place):
    piece = jax.ShapeDtypeStruct((2 * PIECE, QUARTER, LANES), jnp.bfloat16)

    def source(half, i, place):
        return lax.rem(place[1] + i // PIECE + 2 * half, ZL) * PIECE + lax.rem(i, PIECE)

    return pl.pallas_call(
        amplitude_kernel,
        grid_spec=pltpu.PrefetchScalarGridSpec(
            num_scalar_prefetch=1,
            grid=(2 * PIECE,),
            in_specs=[
                pl.BlockSpec((1, PAIRS, NV), lambda i, place: (source(0, i, place), 0, 0)),
                pl.BlockSpec((1, PAIRS, NV), lambda i, place: (source(1, i, place), 0, 0)),
            ],
            out_specs=[pl.BlockSpec((1, QUARTER, LANES), lambda i, place: (i, 0, 0))] * X,
            scratch_shapes=[pltpu.VMEM((NV, LANES), jnp.float32)],
        ),
        out_shape=[piece] * X,
        compiler_params=pltpu.CompilerParams(vmem_limit_bytes=16 * 2**20),
        cost_estimate=pl.CostEstimate(flops=0, bytes_accessed=4 * PAIRS * NV * BLOCK, transcendentals=0),
    )(place, swapped, swapped)


def contract_kernel(*refs):
    left, right, out_ref = refs[:X], refs[X : X + ZL], refs[X + ZL]
    for k in range(X):
        total = jnp.zeros((LANES, 2 * LANES), jnp.float32)
        for j in range(2):
            both = jnp.concatenate([right[j][...], right[j + 2][...]], axis=1)
            total += lax.dot_general(left[k][j], both, (((0,), (0,)), ((), ())), preferred_element_type=jnp.float32)
        out_ref[k] = total[:PAIRS, :LANES] + total[PAIRS:, LANES:]


def contract(left, right):
    left = [part.reshape(2, DEPTH, LANES) for part in left]
    return pl.pallas_call(
        contract_kernel,
        in_specs=[pl.BlockSpec(memory_space=pltpu.VMEM)] * (X + ZL),
        out_specs=pl.BlockSpec(memory_space=pltpu.VMEM),
        out_shape=jax.ShapeDtypeStruct((X, PAIRS, LANES), jnp.float32),
        compiler_params=pltpu.CompilerParams(vmem_limit_bytes=32 * 2**20),
        cost_estimate=pl.CostEstimate(flops=2 * 512 * 3200 * 256, bytes_accessed=5 * 2**20, transcendentals=0),
    )(*left, *right)


def shift_x(array, k):
    return lax.ppermute(array, "x", [(x, (x + k) % X) for x in range(X)])


def shift_zl(array, k):
    return lax.ppermute(array, "zl", [(z, (z - k) % ZL) for z in range(ZL)])


def run(twice_x, twice_z, amplitudes, integrals, owners, offsets):
    x, zl = lax.axis_index("x"), lax.axis_index("zl")
    owner_x, owner_z = owners // ZL, owners % ZL
    place = jnp.stack([x, zl]).astype(jnp.int32)

    if twice_x:
        starts = [offsets[0], offsets[1]]
    else:
        starts = [jnp.where(x * ZL + zl == owners[1], offsets[1], offsets[0])]
    panels = [lax.dynamic_slice_in_dim(integrals, start, PR, 0) for start in starts]
    sent = [jnp.transpose(panel.reshape(PR, PIECE, X, NV), (2, 1, 0, 3)) for panel in panels]
    sent = sent[0][:, None] if len(sent) == 1 else jnp.stack(sent, axis=1)
    got = lax.all_to_all(sent, "x", 0, 0, tiled=True)

    left = turn_amplitudes(jnp.transpose(amplitudes, (2, 0, 1)), place)
    got, left = lax.optimization_barrier((got, left))
    left = [left[0]] + [shift_x(left[k], k) for k in range(1, X)]

    per = len(starts)
    flat = got.reshape(X * per, PIECE // 2, LANES, NV)
    place_of = [owner_x[p] * per + (p if twice_x else 0) for p in range(STEPS)]
    if twice_z:
        sources = jnp.stack(place_of)
    else:
        sources = jnp.where(zl == owner_z[1], place_of[1], place_of[0])[None]
    turned = turn_panel(flat, sources.astype(jnp.int32))
    count = turned.shape[0]
    turned = turned.reshape(count, PIECE // 2, ROWS, ZL, PIECE, LANES)
    sent = jnp.transpose(turned, (3, 2, 0, 1, 4, 5)).reshape(ZL * ROWS, count * PIECE * PIECE // 2, LANES)
    got = lax.all_to_all(sent, ("zl",) + ROW, 0, 0, tiled=True)
    got = got.reshape(ZL, ROWS, count, PIECE // 2, PIECE, 2, PR)
    mine = jnp.stack([
        lax.dynamic_index_in_dim(got, owner_z[p], 0, keepdims=False)[:, p if twice_z else 0] for p in range(STEPS)
    ])
    mine = jnp.transpose(mine, (3, 1, 2, 4, 0, 5)).reshape(DEPTH, LANES)
    right = [mine] + [shift_zl(mine, k) for k in range(1, ZL)]

    part = contract(left, right)
    total = part[0]
    for k in range(1, X):
        total = total + shift_x(part[k], -k)
    spread = lax.all_to_all(total.reshape(ROWS, PAIRS // ROWS, LANES), ROW, 0, 0, tiled=True)
    return jnp.sum(spread, axis=0)


def local(amplitudes, integrals, owners, offsets):
    same_owner = owners[0] == owners[1]
    same_z = owners[0] % ZL == owners[1] % ZL
    case = jnp.where(same_owner, 2, jnp.where(same_z, 1, 0))
    ways = [functools.partial(run, False, False), functools.partial(run, False, True), functools.partial(run, True, True)]
    return lax.switch(case, ways, amplitudes, integrals, owners, offsets)


def solution(mesh):
    fine = Mesh(mesh.devices.reshape(2, 4, 2, X, ZL), ROW + COL)
    in_specs = (P(COL, None, ROW), P(COL, ROW, None), P(), P())
    out_specs = P(COL + ROW, None)
    return jax.shard_map(local, mesh=fine, in_specs=in_specs, out_specs=out_specs, check_vma=False)
```

```python
import jax
import jax.numpy as jnp
from jax import lax
from jax.experimental import pallas as pl
from jax.experimental.pallas import tpu as pltpu
from jax.sharding import Mesh
from jax.sharding import PartitionSpec as P

PR = 64
STEPS = 2
X = 4
ZL = 4
ROW = ("zh", "y", "core")
COL = ("x", "zl")
ROWS = 16
NV = 640
BLOCK = 40
PIECE = 10
HALF = PIECE // 2
PAIRS = 64
LANES = 128
QUARTER = NV // X
DEPTH = PIECE * QUARTER
CHUNK = 16
MESSAGE = 56


def cost(flops, moved):
    return pl.CostEstimate(flops=flops, bytes_accessed=moved, transcendentals=0)


def slice_kernel(owners_ref, offsets_ref, integrals_ref, *refs):
    out_refs, (held, rows, sems) = refs[:X], refs[X:]
    i = pl.program_id(0)
    x = lax.axis_index("x")
    owns_second = jnp.logical_and(x * ZL + lax.axis_index("zl") == owners_ref[1], owners_ref[0] != owners_ref[1])
    start = jnp.where(owns_second, offsets_ref[1], offsets_ref[0])

    def copy(chunk):
        source = integrals_ref.at[pl.ds(start + chunk * CHUNK, CHUNK)]
        return pltpu.make_async_copy(source, held.at[chunk], sems.at[chunk])

    @pl.when(i == 0)
    def _():
        for chunk in range(PR // CHUNK):
            copy(chunk).start()

    for chunk in range(PR // CHUNK):

        @pl.when(i == chunk)
        def _():
            copy(chunk).wait()

    for t in range(NV // LANES):
        lanes = slice(t * LANES, (t + 1) * LANES)
        rows[...] = held[i, :, :, lanes].astype(jnp.float32).reshape(CHUNK * BLOCK, LANES)
        for k in range(X):
            first = lax.rem(x + k, X) * PIECE
            for m in range(PIECE):
                out_refs[k][m, :, lanes] = rows[pl.ds(first + m, CHUNK, stride=BLOCK), :].astype(jnp.bfloat16)


def slice_panel(integrals, owners, offsets):
    piece = jax.ShapeDtypeStruct((PIECE, PR, NV), jnp.bfloat16)
    return pl.pallas_call(
        slice_kernel,
        grid_spec=pltpu.PrefetchScalarGridSpec(
            num_scalar_prefetch=2,
            grid=(PR // CHUNK,),
            in_specs=[pl.BlockSpec(memory_space=pl.ANY)],
            out_specs=[pl.BlockSpec((PIECE, CHUNK, NV), lambda i, owners, offsets: (0, i, 0))] * X,
            scratch_shapes=[
                pltpu.VMEM((PR // CHUNK, CHUNK, BLOCK, NV), jnp.bfloat16),
                pltpu.VMEM((CHUNK * BLOCK, LANES), jnp.float32),
                pltpu.SemaphoreType.DMA((PR // CHUNK,)),
            ],
        ),
        out_shape=[piece] * X,
        compiler_params=pltpu.CompilerParams(vmem_limit_bytes=24 * 2**20),
        cost_estimate=cost(0, 4 * PR * BLOCK * NV),
    )(owners, offsets, integrals)


def turn_kernel(choice_ref, *refs):
    piece_refs, out_ref, (held, turned, message, sem) = refs[: X + 1], refs[X + 1], refs[X + 2 :]
    for k in range(X + 1):

        @pl.when(choice_ref[0] == k)
        def _():
            copy = pltpu.make_async_copy(piece_refs[k], held, sem)
            copy.start()
            copy.wait()

    for half in range(HALF):
        turned[half * NV : (half + 1) * NV, :] = held[half].T.astype(jnp.float32)
    message[...] = jnp.zeros_like(message)
    for half in range(HALF):
        for e in range(PIECE):
            rows = turned[pl.ds(half * NV + e, ROWS * ZL, stride=PIECE), :]
            message[pl.ds(half * PIECE + e, ROWS * ZL, stride=MESSAGE), :] = rows
    out_ref[...] = message[...].astype(jnp.bfloat16).reshape(ROWS * ZL, MESSAGE, LANES)


def turn_panel(choice, pieces):
    pieces = [piece.reshape(HALF, LANES, NV) for piece in pieces]
    return pl.pallas_call(
        turn_kernel,
        grid_spec=pltpu.PrefetchScalarGridSpec(
            num_scalar_prefetch=1,
            grid=(1,),
            in_specs=[pl.BlockSpec(memory_space=pl.ANY)] * (X + 1),
            out_specs=pl.BlockSpec((ROWS * ZL, MESSAGE, LANES), lambda i, choice: (0, 0, 0)),
            scratch_shapes=[
                pltpu.VMEM((HALF, LANES, NV), jnp.bfloat16),
                pltpu.VMEM((HALF * NV, LANES), jnp.float32),
                pltpu.VMEM((ROWS * ZL * MESSAGE, LANES), jnp.float32),
                pltpu.SemaphoreType.DMA,
            ],
        ),
        out_shape=jax.ShapeDtypeStruct((ROWS * ZL, MESSAGE, LANES), jnp.bfloat16),
        compiler_params=pltpu.CompilerParams(vmem_limit_bytes=24 * 2**20),
        cost_estimate=cost(0, 4 * LANES * NV * HALF),
    )(choice[None].astype(jnp.int32), *pieces)


def amplitude_kernel(place_ref, first_ref, second_ref, *refs):
    out_refs, held = refs[:-1], refs[-1]
    stacked = jnp.concatenate([first_ref[0], second_ref[0]], axis=0)
    held[...] = stacked.T.astype(jnp.float32)
    for k in range(X):
        first = lax.rem(place_ref[0] + k, X) * PIECE
        for m in range(PIECE):
            rows = held[pl.ds(first + m, ROWS, stride=BLOCK), :]
            out_ref = out_refs[k] if len(out_refs) > 1 else out_refs[0].at[k]
            out_ref[0, m % 2, m // 2 * ROWS : (m // 2 + 1) * ROWS] = rows.astype(jnp.bfloat16)


def turn_amplitudes(swapped, place, apart):
    piece = (PIECE, 2, QUARTER // 2, LANES)
    if apart:
        shapes = [jax.ShapeDtypeStruct(piece, jnp.bfloat16)] * X
        specs = [pl.BlockSpec((1, 2, QUARTER // 2, LANES), lambda i, place: (i, 0, 0, 0))] * X
    else:
        shapes = jax.ShapeDtypeStruct((X,) + piece, jnp.bfloat16)
        specs = pl.BlockSpec((X, 1, 2, QUARTER // 2, LANES), lambda i, place: (0, i, 0, 0, 0))
    return pl.pallas_call(
        amplitude_kernel,
        grid_spec=pltpu.PrefetchScalarGridSpec(
            num_scalar_prefetch=1,
            grid=(PIECE,),
            in_specs=[
                pl.BlockSpec((1, PAIRS, NV), lambda i, place: (place[1] * PIECE + i, 0, 0)),
                pl.BlockSpec((1, PAIRS, NV), lambda i, place: (place[2] * PIECE + i, 0, 0)),
            ],
            out_specs=specs,
            scratch_shapes=[pltpu.VMEM((NV, LANES), jnp.float32)],
        ),
        out_shape=shapes,
        compiler_params=pltpu.CompilerParams(vmem_limit_bytes=16 * 2**20),
        cost_estimate=cost(0, 2 * PAIRS * NV * BLOCK),
    )(place, swapped, swapped)


def join_kernel(source_ref, first_ref, second_ref, out_ref, low_held, high_held):
    first, second = first_ref[:, 0].astype(jnp.float32), second_ref[:, 0].astype(jnp.float32)
    low = lax.broadcasted_iota(jnp.int32, first.shape, 2) < PR
    low_held[...] = jnp.where(low, first, pltpu.roll(second, PR, 2)).reshape(ROWS * MESSAGE, LANES)
    high_held[...] = jnp.where(low, pltpu.roll(first, PR, 2), second).reshape(ROWS * MESSAGE, LANES)
    for e in range(PIECE):
        for side, held in enumerate((low_held, high_held)):
            for half in range(HALF):
                rows = held[pl.ds(half * PIECE + e, ROWS, stride=MESSAGE), :]
                out_ref[e, side, half * ROWS : (half + 1) * ROWS] = rows.astype(jnp.bfloat16)


def join_panels(got, sources):
    return pl.pallas_call(
        join_kernel,
        grid_spec=pltpu.PrefetchScalarGridSpec(
            num_scalar_prefetch=1,
            grid=(1,),
            in_specs=[
                pl.BlockSpec((ROWS, 1, MESSAGE, LANES), lambda i, source: (0, source[0], 0, 0)),
                pl.BlockSpec((ROWS, 1, MESSAGE, LANES), lambda i, source: (0, source[1], 0, 0)),
            ],
            out_specs=pl.BlockSpec((PIECE, 2, QUARTER // 2, LANES), lambda i, source: (0, 0, 0, 0)),
            scratch_shapes=[pltpu.VMEM((ROWS * MESSAGE, LANES), jnp.float32)] * 2,
        ),
        out_shape=jax.ShapeDtypeStruct((PIECE, 2, QUARTER // 2, LANES), jnp.bfloat16),
        compiler_params=pltpu.CompilerParams(vmem_limit_bytes=16 * 2**20),
        cost_estimate=cost(0, 3 * DEPTH * LANES * 2),
    )(sources, got, got)


def contract_kernel(*refs):
    left, (own_ref, other_ref), out_ref = refs[: 2 * X], refs[2 * X : 2 * X + 2], refs[2 * X + 2]
    both = jnp.concatenate([own_ref[...], other_ref[...]], axis=1)
    for k in range(2 * X):
        total = lax.dot_general(left[k][...], both, (((0,), (0,)), ((), ())), preferred_element_type=jnp.float32)
        out_ref[k // 2, k % 2] = total[:PAIRS, :LANES] + total[PAIRS:, LANES:]


def contract(left, right):
    left = [part.reshape(DEPTH, LANES) for part in left]
    right = [part.reshape(DEPTH, LANES) for part in right]
    return pl.pallas_call(
        contract_kernel,
        in_specs=[pl.BlockSpec(memory_space=pltpu.VMEM)] * (2 * X + 2),
        out_specs=pl.BlockSpec(memory_space=pltpu.VMEM),
        out_shape=jax.ShapeDtypeStruct((X, 2, PAIRS, LANES), jnp.float32),
        compiler_params=pltpu.CompilerParams(vmem_limit_bytes=32 * 2**20),
        cost_estimate=cost(2 * 1024 * 1600 * 256, 5 * 2**20),
    )(*left, *right)


def shift_x(array, k):
    return lax.ppermute(array, "x", [(x, (x + k) % X) for x in range(X)])


def swap_zl(array, bit):
    return lax.ppermute(array, "zl", [(z, z ^ bit) for z in range(ZL)])


def over_x(integrals, owners, offsets):
    pieces = slice_panel(integrals, owners, offsets)
    return [pieces[0]] + [shift_x(pieces[k], k) for k in range(1, X)]


def local(amplitudes, integrals, owners, offsets):
    got = over_x(integrals, owners, offsets)

    x, zl = lax.axis_index("x"), lax.axis_index("zl")
    owner_x, owner_z = lax.shift_right_logical(owners, 2), lax.bitwise_and(owners, 3)
    same_owner = owners[0] == owners[1]
    same_z = owner_z[0] == owner_z[1]
    at_z = [owner_z[0], jnp.where(same_z, lax.bitwise_xor(owner_z[1], 1), owner_z[1])]
    distance = lax.bitwise_and(x - owner_x, 3)
    choice = jnp.where(zl == at_z[1], jnp.where(same_z, X, distance[1]), distance[0])

    swapped = jnp.transpose(amplitudes, (2, 0, 1))
    places = [jnp.stack([x, lax.bitwise_xor(zl, k), lax.bitwise_xor(zl, k + 2)]).astype(jnp.int32) for k in range(2)]
    others = swap_zl(turn_amplitudes(swapped, places[1], False), 1)
    owns = turn_amplitudes(swapped, places[0], True)
    got, owns = lax.optimization_barrier((got, owns))

    def stay(*operands):
        return jnp.zeros((PIECE, PR, NV), jnp.bfloat16)

    def move(same_owner, owners, offsets, place, integrals, *got):
        def again(owners, offsets, integrals, *got):
            return over_x(integrals, owners, jnp.stack([offsets[1], offsets[1]]))

        def keep(owners, offsets, integrals, *got):
            return list(got)

        got = lax.cond(same_owner, again, keep, owners, offsets, integrals, *got)
        return swap_zl(lax.select_n(place, *got), 1)

    moved = lax.cond(same_z, move, stay, same_owner, owners, offsets, distance[1], integrals, *got)

    left = [owns[0], others[0]]
    for k in range(1, X):
        left += [shift_x(owns[k], k), shift_x(others[k], k)]

    message = turn_panel(choice, got + [moved])
    spread = lax.all_to_all(message, ROW + ("zl",), 0, 0, tiled=True)
    mine = join_panels(spread.reshape(ROWS, ZL, MESSAGE, LANES), jnp.stack(at_z).astype(jnp.int32))
    part = contract(left, [mine, swap_zl(mine, 2)])

    total = part[0]
    for k in range(1, X):
        total = total + shift_x(part[k], -k)
    total = total[0] + swap_zl(total[1], 1)
    spread = lax.all_to_all(total.reshape(ROWS, PAIRS // ROWS, LANES), ROW, 0, 0, tiled=True)
    return jnp.sum(spread, axis=0)


def solution(mesh):
    fine = Mesh(mesh.devices.reshape(2, 4, 2, X, ZL), ROW + COL)
    in_specs = (P(COL, None, ROW), P(COL, ROW, None), P(), P())
    out_specs = P(COL + ROW, None)
    return jax.shard_map(local, mesh=fine, in_specs=in_specs, out_specs=out_specs, check_vma=False)
```

```python
import jax
import jax.numpy as jnp
from jax import lax
from jax.experimental import pallas as pl
from jax.experimental.pallas import tpu as pltpu
from jax.sharding import Mesh
from jax.sharding import PartitionSpec as P

PR = 64
STEPS = 2
X = 4
ZL = 4
ROW = ("zh", "y", "core")
Z = ("za", "zb")
COL = ("x",) + Z
ROWS = 16
NV = 640
BLOCK = 40
PIECE = 10
HALF = PIECE // 2
PAIRS = 64
LANES = 128
QUARTER = NV // X
DEPTH = PIECE * QUARTER
CHUNK = 16
MESSAGE = 56


def cost(flops, moved):
    return pl.CostEstimate(flops=flops, bytes_accessed=moved, transcendentals=0)


def slice_kernel(owners_ref, offsets_ref, integrals_ref, *refs):
    out_refs, (held, rows, sems) = refs[:X], refs[X:]
    i = pl.program_id(0)
    x = lax.axis_index("x")
    owns_second = jnp.logical_and(x * ZL + 2 * lax.axis_index("za") + lax.axis_index("zb") == owners_ref[1], owners_ref[0] != owners_ref[1])
    start = jnp.where(owns_second, offsets_ref[1], offsets_ref[0])

    def copy(chunk):
        source = integrals_ref.at[pl.ds(start + chunk * CHUNK, CHUNK)]
        return pltpu.make_async_copy(source, held.at[chunk], sems.at[chunk])

    @pl.when(i == 0)
    def _():
        for chunk in range(PR // CHUNK):
            copy(chunk).start()

    for chunk in range(PR // CHUNK):

        @pl.when(i == chunk)
        def _():
            copy(chunk).wait()

    for t in range(NV // LANES):
        lanes = slice(t * LANES, (t + 1) * LANES)
        rows[...] = held[i, :, :, lanes].astype(jnp.float32).reshape(CHUNK * BLOCK, LANES)
        for k in range(X):
            first = lax.rem(x + k, X) * PIECE
            for m in range(PIECE):
                out_refs[k][m, :, lanes] = rows[pl.ds(first + m, CHUNK, stride=BLOCK), :].astype(jnp.bfloat16)


def slice_panel(integrals, owners, offsets):
    piece = jax.ShapeDtypeStruct((PIECE, PR, NV), jnp.bfloat16)
    return pl.pallas_call(
        slice_kernel,
        grid_spec=pltpu.PrefetchScalarGridSpec(
            num_scalar_prefetch=2,
            grid=(PR // CHUNK,),
            in_specs=[pl.BlockSpec(memory_space=pl.ANY)],
            out_specs=[pl.BlockSpec((PIECE, CHUNK, NV), lambda i, owners, offsets: (0, i, 0))] * X,
            scratch_shapes=[
                pltpu.VMEM((PR // CHUNK, CHUNK, BLOCK, NV), jnp.bfloat16),
                pltpu.VMEM((CHUNK * BLOCK, LANES), jnp.float32),
                pltpu.SemaphoreType.DMA((PR // CHUNK,)),
            ],
        ),
        out_shape=[piece] * X,
        compiler_params=pltpu.CompilerParams(vmem_limit_bytes=24 * 2**20),
        cost_estimate=cost(0, 4 * PR * BLOCK * NV),
    )(owners, offsets, integrals)


def turn_kernel(choice_ref, *refs):
    piece_refs, out_ref, (held, turned, message, sem) = refs[: X + 1], refs[X + 1], refs[X + 2 :]
    for k in range(X + 1):

        @pl.when(choice_ref[0] == k)
        def _():
            copy = pltpu.make_async_copy(piece_refs[k], held, sem)
            copy.start()
            copy.wait()

    for half in range(HALF):
        turned[half * NV : (half + 1) * NV, :] = held[half].T.astype(jnp.float32)
    message[...] = jnp.zeros_like(message)
    for half in range(HALF):
        for e in range(PIECE):
            rows = turned[pl.ds(half * NV + e, ROWS * ZL, stride=PIECE), :]
            message[pl.ds(half * PIECE + e, ROWS * ZL, stride=MESSAGE), :] = rows
    out_ref[...] = message[...].astype(jnp.bfloat16).reshape(ROWS * ZL, MESSAGE, LANES)


def turn_panel(choice, pieces):
    pieces = [piece.reshape(HALF, LANES, NV) for piece in pieces]
    return pl.pallas_call(
        turn_kernel,
        grid_spec=pltpu.PrefetchScalarGridSpec(
            num_scalar_prefetch=1,
            grid=(1,),
            in_specs=[pl.BlockSpec(memory_space=pl.ANY)] * (X + 1),
            out_specs=pl.BlockSpec((ROWS * ZL, MESSAGE, LANES), lambda i, choice: (0, 0, 0)),
            scratch_shapes=[
                pltpu.VMEM((HALF, LANES, NV), jnp.bfloat16),
                pltpu.VMEM((HALF * NV, LANES), jnp.float32),
                pltpu.VMEM((ROWS * ZL * MESSAGE, LANES), jnp.float32),
                pltpu.SemaphoreType.DMA,
            ],
        ),
        out_shape=jax.ShapeDtypeStruct((ROWS * ZL, MESSAGE, LANES), jnp.bfloat16),
        compiler_params=pltpu.CompilerParams(vmem_limit_bytes=24 * 2**20),
        cost_estimate=cost(0, 4 * LANES * NV * HALF),
    )(choice[None].astype(jnp.int32), *pieces)


def amplitude_kernel(place_ref, first_ref, second_ref, *refs):
    out_refs, held = refs[:-1], refs[-1]
    stacked = jnp.concatenate([first_ref[0], second_ref[0]], axis=0)
    held[...] = stacked.T.astype(jnp.float32)
    for k in range(X):
        first = lax.rem(place_ref[0] + k, X) * PIECE
        for m in range(PIECE):
            rows = held[pl.ds(first + m, ROWS, stride=BLOCK), :]
            out_ref = out_refs[k] if len(out_refs) > 1 else out_refs[0].at[k]
            out_ref[0, m % 2, m // 2 * ROWS : (m // 2 + 1) * ROWS] = rows.astype(jnp.bfloat16)


def turn_amplitudes(swapped, place, apart):
    piece = (PIECE, 2, QUARTER // 2, LANES)
    if apart:
        shapes = [jax.ShapeDtypeStruct(piece, jnp.bfloat16)] * X
        specs = [pl.BlockSpec((1, 2, QUARTER // 2, LANES), lambda i, place: (i, 0, 0, 0))] * X
    else:
        shapes = jax.ShapeDtypeStruct((X,) + piece, jnp.bfloat16)
        specs = pl.BlockSpec((X, 1, 2, QUARTER // 2, LANES), lambda i, place: (0, i, 0, 0, 0))
    return pl.pallas_call(
        amplitude_kernel,
        grid_spec=pltpu.PrefetchScalarGridSpec(
            num_scalar_prefetch=1,
            grid=(PIECE,),
            in_specs=[
                pl.BlockSpec((1, PAIRS, NV), lambda i, place: (place[1] * PIECE + i, 0, 0)),
                pl.BlockSpec((1, PAIRS, NV), lambda i, place: (place[2] * PIECE + i, 0, 0)),
            ],
            out_specs=specs,
            scratch_shapes=[pltpu.VMEM((NV, LANES), jnp.float32)],
        ),
        out_shape=shapes,
        compiler_params=pltpu.CompilerParams(vmem_limit_bytes=16 * 2**20),
        cost_estimate=cost(0, 2 * PAIRS * NV * BLOCK),
    )(place, swapped, swapped)


def join_kernel(source_ref, first_ref, second_ref, out_ref, low_held, high_held):
    first, second = first_ref[:, 0].astype(jnp.float32), second_ref[:, 0].astype(jnp.float32)
    low = lax.broadcasted_iota(jnp.int32, first.shape, 2) < PR
    low_held[...] = jnp.where(low, first, pltpu.roll(second, PR, 2)).reshape(ROWS * MESSAGE, LANES)
    high_held[...] = jnp.where(low, pltpu.roll(first, PR, 2), second).reshape(ROWS * MESSAGE, LANES)
    for e in range(PIECE):
        for side, held in enumerate((low_held, high_held)):
            for half in range(HALF):
                rows = held[pl.ds(half * PIECE + e, ROWS, stride=MESSAGE), :]
                out_ref[e, side, half * ROWS : (half + 1) * ROWS] = rows.astype(jnp.bfloat16)


def join_panels(got, sources):
    return pl.pallas_call(
        join_kernel,
        grid_spec=pltpu.PrefetchScalarGridSpec(
            num_scalar_prefetch=1,
            grid=(1,),
            in_specs=[
                pl.BlockSpec((ROWS, 1, MESSAGE, LANES), lambda i, source: (0, source[0], 0, 0)),
                pl.BlockSpec((ROWS, 1, MESSAGE, LANES), lambda i, source: (0, source[1], 0, 0)),
            ],
            out_specs=pl.BlockSpec((PIECE, 2, QUARTER // 2, LANES), lambda i, source: (0, 0, 0, 0)),
            scratch_shapes=[pltpu.VMEM((ROWS * MESSAGE, LANES), jnp.float32)] * 2,
        ),
        out_shape=jax.ShapeDtypeStruct((PIECE, 2, QUARTER // 2, LANES), jnp.bfloat16),
        compiler_params=pltpu.CompilerParams(vmem_limit_bytes=16 * 2**20),
        cost_estimate=cost(0, 3 * DEPTH * LANES * 2),
    )(sources, got, got)


def contract_kernel(*refs):
    left, (own_ref, other_ref), out_ref = refs[: 2 * X], refs[2 * X : 2 * X + 2], refs[2 * X + 2]
    both = jnp.concatenate([own_ref[...], other_ref[...]], axis=1)
    for k in range(2 * X):
        total = lax.dot_general(left[k][...], both, (((0,), (0,)), ((), ())), preferred_element_type=jnp.float32)
        side = lax.rem(k + lax.axis_index("zb"), 2)
        out_ref[k // 2, side] = total[:PAIRS, :LANES] + total[PAIRS:, LANES:]


def contract(left, right):
    left = [part.reshape(DEPTH, LANES) for part in left]
    right = [part.reshape(DEPTH, LANES) for part in right]
    return pl.pallas_call(
        contract_kernel,
        in_specs=[pl.BlockSpec(memory_space=pltpu.VMEM)] * (2 * X + 2),
        out_specs=pl.BlockSpec(memory_space=pltpu.VMEM),
        out_shape=jax.ShapeDtypeStruct((X, 2, PAIRS, LANES), jnp.float32),
        compiler_params=pltpu.CompilerParams(vmem_limit_bytes=32 * 2**20),
        cost_estimate=cost(2 * 1024 * 1600 * 256, 5 * 2**20),
    )(*left, *right)


def shift_x(array, k):
    return lax.ppermute(array, "x", [(x, (x + k) % X) for x in range(X)])


def swap_zl(array, bit):
    return lax.ppermute(array, Z, [(z, z ^ bit) for z in range(ZL)])


def over_x(integrals, owners, offsets):
    pieces = slice_panel(integrals, owners, offsets)
    return [pieces[0]] + [shift_x(pieces[k], k) for k in range(1, X)]


def local(amplitudes, integrals, owners, offsets):
    got = over_x(integrals, owners, offsets)

    x, zl = lax.axis_index("x"), lax.axis_index(Z)
    owner_x, owner_z = lax.shift_right_logical(owners, 2), lax.bitwise_and(owners, 3)
    same_owner = owners[0] == owners[1]
    same_z = owner_z[0] == owner_z[1]
    at_z = [owner_z[0], jnp.where(same_z, lax.bitwise_xor(owner_z[1], 1), owner_z[1])]
    distance = lax.bitwise_and(x - owner_x, 3)
    choice = jnp.where(zl == at_z[1], jnp.where(same_z, X, distance[1]), distance[0])

    swapped = jnp.transpose(amplitudes, (2, 0, 1))
    places = [jnp.stack([x, lax.bitwise_xor(zl, k), lax.bitwise_xor(zl, k + 2)]).astype(jnp.int32) for k in range(2)]
    others = swap_zl(turn_amplitudes(swapped, places[1], False), 1)
    owns = turn_amplitudes(swapped, places[0], True)
    got, owns = lax.optimization_barrier((got, owns))

    def stay(*operands):
        return jnp.zeros((PIECE, PR, NV), jnp.bfloat16)

    def move(place, owners, offsets, integrals, *got):
        return swap_zl(lax.select_n(place, *got), 1)

    def again(place, owners, offsets, integrals, *got):
        got = over_x(integrals, owners, jnp.stack([offsets[1], offsets[1]]))
        return swap_zl(lax.select_n(place, *got), 1)

    case = jnp.where(same_owner, 2, jnp.where(same_z, 1, 0))
    moved = lax.switch(case, [stay, move, again], distance[1], owners, offsets, integrals, *got)

    left = [owns[0], others[0]]
    for k in range(1, X):
        left += [shift_x(owns[k], k), shift_x(others[k], k)]

    message = turn_panel(choice, got + [moved])
    spread = lax.all_to_all(message, ROW + Z, 0, 0, tiled=True)
    mine = join_panels(spread.reshape(ROWS, ZL, MESSAGE, LANES), jnp.stack(at_z).astype(jnp.int32))
    part = contract(left, [mine, swap_zl(mine, 2)])

    total = part[0]
    for k in range(1, X):
        total = total + shift_x(part[k], -k)
    spread = lax.all_to_all(total.reshape(2 * ROWS, PAIRS // ROWS, LANES), ("zb",) + ROW, 0, 0, tiled=True)
    return jnp.sum(spread, axis=0)


def solution(mesh):
    fine = Mesh(mesh.devices.reshape(2, 4, 2, X, 2, 2), ROW + COL)
    in_specs = (P(COL, None, ROW), P(COL, ROW, None), P(), P())
    out_specs = P(COL + ROW, None)
    return jax.shard_map(local, mesh=fine, in_specs=in_specs, out_specs=out_specs, check_vma=False)
```

```python
import functools

import jax
import jax.numpy as jnp
from jax import lax
from jax.experimental import pallas as pl
from jax.experimental.pallas import tpu as pltpu
from jax.sharding import Mesh
from jax.sharding import PartitionSpec as P

PR = 64
STEPS = 2
X = 4
ZL = 4
ROW = ("zh", "y", "core")
Z = ("za", "zb")
COL = ("x",) + Z
ROWS = 16
NV = 640
BLOCK = 40
PIECE = 10
HALF = PIECE // 2
PAIRS = 64
LANES = 128
QUARTER = NV // X
DEPTH = PIECE * QUARTER
CHUNK = 16
MESSAGE = 56


def cost(flops, moved):
    return pl.CostEstimate(flops=flops, bytes_accessed=moved, transcendentals=0)


def slice_kernel(steps, owners_ref, offsets_ref, integrals_ref, *refs):
    out_refs, (held, rows, sems) = refs[: len(steps)], refs[len(steps) :]
    i = pl.program_id(0)
    x = lax.axis_index("x")
    owns_second = jnp.logical_and(x * ZL + 2 * lax.axis_index("za") + lax.axis_index("zb") == owners_ref[1], owners_ref[0] != owners_ref[1])
    start = jnp.where(owns_second, offsets_ref[1], offsets_ref[0])

    def copy(chunk):
        source = integrals_ref.at[pl.ds(start + chunk * CHUNK, CHUNK)]
        return pltpu.make_async_copy(source, held.at[chunk], sems.at[chunk])

    @pl.when(i == 0)
    def _():
        for chunk in range(PR // CHUNK):
            copy(chunk).start()

    for chunk in range(PR // CHUNK):

        @pl.when(i == chunk)
        def _():
            copy(chunk).wait()

    for t in range(NV // LANES):
        lanes = slice(t * LANES, (t + 1) * LANES)
        rows[...] = held[i, :, :, lanes].astype(jnp.float32).reshape(CHUNK * BLOCK, LANES)
        for out_ref, k in zip(out_refs, steps):
            first = lax.rem(x + k, X) * PIECE
            for m in range(PIECE):
                out_ref[m, :, lanes] = rows[pl.ds(first + m, CHUNK, stride=BLOCK), :].astype(jnp.bfloat16)


def slice_panel(steps, integrals, owners, offsets):
    piece = jax.ShapeDtypeStruct((PIECE, PR, NV), jnp.bfloat16)
    return pl.pallas_call(
        functools.partial(slice_kernel, steps),
        grid_spec=pltpu.PrefetchScalarGridSpec(
            num_scalar_prefetch=2,
            grid=(PR // CHUNK,),
            in_specs=[pl.BlockSpec(memory_space=pl.ANY)],
            out_specs=[pl.BlockSpec((PIECE, CHUNK, NV), lambda i, owners, offsets: (0, i, 0))] * len(steps),
            scratch_shapes=[
                pltpu.VMEM((PR // CHUNK, CHUNK, BLOCK, NV), jnp.bfloat16),
                pltpu.VMEM((CHUNK * BLOCK, LANES), jnp.float32),
                pltpu.SemaphoreType.DMA((PR // CHUNK,)),
            ],
        ),
        out_shape=[piece] * len(steps),
        compiler_params=pltpu.CompilerParams(vmem_limit_bytes=24 * 2**20),
        cost_estimate=cost(0, 4 * PR * BLOCK * NV),
    )(owners, offsets, integrals)


def turn_kernel(choice_ref, *refs):
    piece_refs, out_ref, (held, turned, message, sems) = refs[: X + 1], refs[X + 1], refs[X + 2 :]
    for k in range(X + 1):

        @pl.when(choice_ref[0] == k)
        def _():
            for half in range(HALF):
                pltpu.make_async_copy(piece_refs[k].at[half], held.at[half], sems.at[half]).start()

    message[...] = jnp.zeros_like(message)
    for half in range(HALF):
        pltpu.make_async_copy(piece_refs[0].at[half], held.at[half], sems.at[half]).wait()
        turned[half * NV : (half + 1) * NV, :] = held[half].T.astype(jnp.float32)
    for half in range(HALF):
        for e in range(PIECE):
            rows = turned[pl.ds(half * NV + e, ROWS * ZL, stride=PIECE), :]
            message[pl.ds(half * PIECE + e, ROWS * ZL, stride=MESSAGE), :] = rows
    out_ref[...] = message[...].astype(jnp.bfloat16).reshape(ROWS * ZL, MESSAGE, LANES)


def turn_panel(choice, pieces):
    pieces = [piece.reshape(HALF, LANES, NV) for piece in pieces]
    return pl.pallas_call(
        turn_kernel,
        grid_spec=pltpu.PrefetchScalarGridSpec(
            num_scalar_prefetch=1,
            grid=(1,),
            in_specs=[pl.BlockSpec(memory_space=pl.ANY)] * (X + 1),
            out_specs=pl.BlockSpec((ROWS * ZL, MESSAGE, LANES), lambda i, choice: (0, 0, 0)),
            scratch_shapes=[
                pltpu.VMEM((HALF, LANES, NV), jnp.bfloat16),
                pltpu.VMEM((HALF * NV, LANES), jnp.float32),
                pltpu.VMEM((ROWS * ZL * MESSAGE, LANES), jnp.float32),
                pltpu.SemaphoreType.DMA((HALF,)),
            ],
        ),
        out_shape=jax.ShapeDtypeStruct((ROWS * ZL, MESSAGE, LANES), jnp.bfloat16),
        compiler_params=pltpu.CompilerParams(vmem_limit_bytes=24 * 2**20),
        cost_estimate=cost(0, 4 * LANES * NV * HALF),
    )(choice[None].astype(jnp.int32), *pieces)


def amplitude_kernel(place_ref, first_ref, second_ref, *refs):
    out_refs, held = refs[:-1], refs[-1]
    stacked = jnp.concatenate([first_ref[0], second_ref[0]], axis=0)
    held[...] = stacked.T.astype(jnp.float32)
    for k in range(X):
        first = lax.rem(place_ref[0] + k, X) * PIECE
        for m in range(PIECE):
            rows = held[pl.ds(first + m, ROWS, stride=BLOCK), :]
            out_ref = out_refs[k] if len(out_refs) > 1 else out_refs[0].at[k]
            out_ref[0, m % 2, m // 2 * ROWS : (m // 2 + 1) * ROWS] = rows.astype(jnp.bfloat16)


def turn_amplitudes(swapped, place, apart):
    piece = (PIECE, 2, QUARTER // 2, LANES)
    if apart:
        shapes = [jax.ShapeDtypeStruct(piece, jnp.bfloat16)] * X
        specs = [pl.BlockSpec((1, 2, QUARTER // 2, LANES), lambda i, place: (i, 0, 0, 0))] * X
    else:
        shapes = jax.ShapeDtypeStruct((X,) + piece, jnp.bfloat16)
        specs = pl.BlockSpec((X, 1, 2, QUARTER // 2, LANES), lambda i, place: (0, i, 0, 0, 0))
    return pl.pallas_call(
        amplitude_kernel,
        grid_spec=pltpu.PrefetchScalarGridSpec(
            num_scalar_prefetch=1,
            grid=(PIECE,),
            in_specs=[
                pl.BlockSpec((1, PAIRS, NV), lambda i, place: (place[1] * PIECE + i, 0, 0)),
                pl.BlockSpec((1, PAIRS, NV), lambda i, place: (place[2] * PIECE + i, 0, 0)),
            ],
            out_specs=specs,
            scratch_shapes=[pltpu.VMEM((NV, LANES), jnp.float32)],
        ),
        out_shape=shapes,
        compiler_params=pltpu.CompilerParams(vmem_limit_bytes=16 * 2**20),
        cost_estimate=cost(0, 2 * PAIRS * NV * BLOCK),
    )(place, swapped, swapped)


def join_kernel(source_ref, first_ref, second_ref, out_ref, low_held, high_held):
    first, second = first_ref[:, 0].astype(jnp.float32), second_ref[:, 0].astype(jnp.float32)
    low = lax.broadcasted_iota(jnp.int32, first.shape, 2) < PR
    low_held[...] = jnp.where(low, first, pltpu.roll(second, PR, 2)).reshape(ROWS * MESSAGE, LANES)
    high_held[...] = jnp.where(low, pltpu.roll(first, PR, 2), second).reshape(ROWS * MESSAGE, LANES)
    for e in range(PIECE):
        for side, held in enumerate((low_held, high_held)):
            for half in range(HALF):
                rows = held[pl.ds(half * PIECE + e, ROWS, stride=MESSAGE), :]
                out_ref[e, side, half * ROWS : (half + 1) * ROWS] = rows.astype(jnp.bfloat16)


def join_panels(got, sources):
    return pl.pallas_call(
        join_kernel,
        grid_spec=pltpu.PrefetchScalarGridSpec(
            num_scalar_prefetch=1,
            grid=(1,),
            in_specs=[
                pl.BlockSpec((ROWS, 1, MESSAGE, LANES), lambda i, source: (0, source[0], 0, 0)),
                pl.BlockSpec((ROWS, 1, MESSAGE, LANES), lambda i, source: (0, source[1], 0, 0)),
            ],
            out_specs=pl.BlockSpec((PIECE, 2, QUARTER // 2, LANES), lambda i, source: (0, 0, 0, 0)),
            scratch_shapes=[pltpu.VMEM((ROWS * MESSAGE, LANES), jnp.float32)] * 2,
        ),
        out_shape=jax.ShapeDtypeStruct((PIECE, 2, QUARTER // 2, LANES), jnp.bfloat16),
        compiler_params=pltpu.CompilerParams(vmem_limit_bytes=16 * 2**20),
        cost_estimate=cost(0, 3 * DEPTH * LANES * 2),
    )(sources, got, got)


def contract_kernel(*refs):
    left, (own_ref, other_ref), out_ref = refs[: 2 * X], refs[2 * X : 2 * X + 2], refs[2 * X + 2]
    both = jnp.concatenate([own_ref[...], other_ref[...]], axis=1)
    for k in range(2 * X):
        total = lax.dot_general(left[k][...], both, (((0,), (0,)), ((), ())), preferred_element_type=jnp.float32)
        side = lax.rem(k + lax.axis_index("zb"), 2)
        out_ref[k // 2, side] = total[:PAIRS, :LANES] + total[PAIRS:, LANES:]


def contract(left, right):
    left = [part.reshape(DEPTH, LANES) for part in left]
    right = [part.reshape(DEPTH, LANES) for part in right]
    return pl.pallas_call(
        contract_kernel,
        in_specs=[pl.BlockSpec(memory_space=pltpu.VMEM)] * (2 * X + 2),
        out_specs=pl.BlockSpec(memory_space=pltpu.VMEM),
        out_shape=jax.ShapeDtypeStruct((X, 2, PAIRS, LANES), jnp.float32),
        compiler_params=pltpu.CompilerParams(vmem_limit_bytes=32 * 2**20),
        cost_estimate=cost(2 * 1024 * 1600 * 256, 5 * 2**20),
    )(*left, *right)


def shift_x(array, k):
    return lax.ppermute(array, "x", [(x, (x + k) % X) for x in range(X)])


def swap_zl(array, bit):
    return lax.ppermute(array, Z, [(z, z ^ bit) for z in range(ZL)])


def over_x(integrals, owners, offsets):
    pieces = slice_panel((1, 2, 3), integrals, owners, offsets)
    got = [shift_x(pieces[k - 1], k) for k in range(1, X)]
    owners, _ = lax.optimization_barrier((owners, pieces[0]))
    return list(slice_panel((0,), integrals, owners, offsets)) + got


def local(amplitudes, integrals, owners, offsets):
    got = over_x(integrals, owners, offsets)

    x, zl = lax.axis_index("x"), lax.axis_index(Z)
    owner_x, owner_z = lax.shift_right_logical(owners, 2), lax.bitwise_and(owners, 3)
    same_owner = owners[0] == owners[1]
    same_z = owner_z[0] == owner_z[1]
    at_z = [owner_z[0], jnp.where(same_z, lax.bitwise_xor(owner_z[1], 1), owner_z[1])]
    distance = lax.bitwise_and(x - owner_x, 3)
    choice = jnp.where(zl == at_z[1], jnp.where(same_z, X, distance[1]), distance[0])

    swapped = jnp.transpose(amplitudes, (2, 0, 1))
    places = [jnp.stack([x, lax.bitwise_xor(zl, k), lax.bitwise_xor(zl, k + 2)]).astype(jnp.int32) for k in range(2)]
    others = swap_zl(turn_amplitudes(swapped, places[1], False), 1)
    owns = turn_amplitudes(swapped, places[0], True)
    got, owns = lax.optimization_barrier((got, owns))

    def stay(*operands):
        return pl.pallas_call(
            lambda out_ref: None,
            out_specs=pl.BlockSpec(memory_space=pl.ANY),
            out_shape=jax.ShapeDtypeStruct((PIECE, PR, NV), jnp.bfloat16),
        )()

    def move(place, owners, offsets, integrals, *got):
        return swap_zl(lax.select_n(place, *got), 1)

    def again(place, owners, offsets, integrals, *got):
        got = over_x(integrals, owners, jnp.stack([offsets[1], offsets[1]]))
        return swap_zl(lax.select_n(place, *got), 1)

    case = jnp.where(same_owner, 2, jnp.where(same_z, 1, 0))
    moved = lax.switch(case, [stay, move, again], distance[1], owners, offsets, integrals, *got)

    left = [owns[0], others[0]]
    for k in range(1, X):
        left += [shift_x(owns[k], k), shift_x(others[k], k)]

    message = turn_panel(choice, got + [moved])
    spread = lax.all_to_all(message, ROW + Z, 0, 0, tiled=True)
    mine = join_panels(spread.reshape(ROWS, ZL, MESSAGE, LANES), jnp.stack(at_z).astype(jnp.int32))
    part = contract(left, [mine, swap_zl(mine, 2)])

    total = part[0]
    for k in range(1, X):
        total = total + shift_x(part[k], -k)
    spread = lax.all_to_all(total.reshape(2 * ROWS, PAIRS // ROWS, LANES), ("zb",) + ROW, 0, 0, tiled=True)
    return jnp.sum(spread, axis=0)


def solution(mesh):
    fine = Mesh(mesh.devices.reshape(2, 4, 2, X, 2, 2), ROW + COL)
    in_specs = (P(COL, None, ROW), P(COL, ROW, None), P(), P())
    out_specs = P(COL + ROW, None)
    return jax.shard_map(local, mesh=fine, in_specs=in_specs, out_specs=out_specs, check_vma=False)
```

```python
import functools

import jax
import jax.numpy as jnp
from jax import lax
from jax.experimental import pallas as pl
from jax.experimental.pallas import tpu as pltpu
from jax.sharding import Mesh
from jax.sharding import PartitionSpec as P

PR = 64
STEPS = 2
X = 4
ZL = 4
ROW = ("zh", "y", "core")
Z = ("za", "zb")
COL = ("x",) + Z
ROWS = 16
NV = 640
BLOCK = 40
PIECE = 10
HALF = PIECE // 2
PAIRS = 64
LANES = 128
QUARTER = NV // X
DEPTH = PIECE * QUARTER
CHUNK = 16
MESSAGE = 56


def cost(flops, moved):
    return pl.CostEstimate(flops=flops, bytes_accessed=moved, transcendentals=0)


def slice_kernel(steps, owners_ref, offsets_ref, integrals_ref, *refs):
    out_refs, (held, rows, sems) = refs[: len(steps)], refs[len(steps) :]
    i = pl.program_id(0)
    x = lax.axis_index("x")
    owns_second = jnp.logical_and(x * ZL + 2 * lax.axis_index("za") + lax.axis_index("zb") == owners_ref[1], owners_ref[0] != owners_ref[1])
    start = jnp.where(owns_second, offsets_ref[1], offsets_ref[0])

    def copy(chunk):
        source = integrals_ref.at[pl.ds(start + chunk * CHUNK, CHUNK)]
        return pltpu.make_async_copy(source, held.at[chunk], sems.at[chunk])

    @pl.when(i == 0)
    def _():
        for chunk in range(PR // CHUNK):
            copy(chunk).start()

    for chunk in range(PR // CHUNK):

        @pl.when(i == chunk)
        def _():
            copy(chunk).wait()

    for t in range(NV // LANES):
        lanes = slice(t * LANES, (t + 1) * LANES)
        rows[...] = held[i, :, :, lanes].astype(jnp.float32).reshape(CHUNK * BLOCK, LANES)
        for out_ref, k in zip(out_refs, steps):
            first = lax.rem(x + k, X) * PIECE
            for m in range(PIECE):
                out_ref[m, :, lanes] = rows[pl.ds(first + m, CHUNK, stride=BLOCK), :].astype(jnp.bfloat16)


def slice_panel(steps, integrals, owners, offsets):
    piece = jax.ShapeDtypeStruct((PIECE, PR, NV), jnp.bfloat16)
    return pl.pallas_call(
        functools.partial(slice_kernel, steps),
        grid_spec=pltpu.PrefetchScalarGridSpec(
            num_scalar_prefetch=2,
            grid=(PR // CHUNK,),
            in_specs=[pl.BlockSpec(memory_space=pl.ANY)],
            out_specs=[pl.BlockSpec((PIECE, CHUNK, NV), lambda i, owners, offsets: (0, i, 0))] * len(steps),
            scratch_shapes=[
                pltpu.VMEM((PR // CHUNK, CHUNK, BLOCK, NV), jnp.bfloat16),
                pltpu.VMEM((CHUNK * BLOCK, LANES), jnp.float32),
                pltpu.SemaphoreType.DMA((PR // CHUNK,)),
            ],
        ),
        out_shape=[piece] * len(steps),
        compiler_params=pltpu.CompilerParams(vmem_limit_bytes=24 * 2**20),
        cost_estimate=cost(0, 4 * PR * BLOCK * NV),
    )(owners, offsets, integrals)


def turn_kernel(choice_ref, *refs):
    piece_refs, out_ref, (held, turned, message, sems) = refs[: X + 1], refs[X + 1], refs[X + 2 :]
    for k in range(X + 1):

        @pl.when(choice_ref[0] == k)
        def _():
            for half in range(HALF):
                pltpu.make_async_copy(piece_refs[k].at[half], held.at[half], sems.at[half]).start()

    message[...] = jnp.zeros_like(message)
    for half in range(HALF):
        pltpu.make_async_copy(piece_refs[0].at[half], held.at[half], sems.at[half]).wait()
        turned[half * NV : (half + 1) * NV, :] = held[half].T.astype(jnp.float32)
    for half in range(HALF):
        for e in range(PIECE):
            rows = turned[pl.ds(half * NV + e, ROWS * ZL, stride=PIECE), :]
            message[pl.ds(half * PIECE + e, ROWS * ZL, stride=MESSAGE), :] = rows
    out_ref[...] = message[...].astype(jnp.bfloat16).reshape(ROWS * ZL, MESSAGE, LANES)


def turn_panel(choice, pieces):
    pieces = [piece.reshape(HALF, LANES, NV) for piece in pieces]
    return pl.pallas_call(
        turn_kernel,
        grid_spec=pltpu.PrefetchScalarGridSpec(
            num_scalar_prefetch=1,
            grid=(1,),
            in_specs=[pl.BlockSpec(memory_space=pl.ANY)] * (X + 1),
            out_specs=pl.BlockSpec((ROWS * ZL, MESSAGE, LANES), lambda i, choice: (0, 0, 0)),
            scratch_shapes=[
                pltpu.VMEM((HALF, LANES, NV), jnp.bfloat16),
                pltpu.VMEM((HALF * NV, LANES), jnp.float32),
                pltpu.VMEM((ROWS * ZL * MESSAGE, LANES), jnp.float32),
                pltpu.SemaphoreType.DMA((HALF,)),
            ],
        ),
        out_shape=jax.ShapeDtypeStruct((ROWS * ZL, MESSAGE, LANES), jnp.bfloat16),
        compiler_params=pltpu.CompilerParams(vmem_limit_bytes=24 * 2**20),
        cost_estimate=cost(0, 4 * LANES * NV * HALF),
    )(choice[None].astype(jnp.int32), *pieces)


def amplitude_kernel(place_ref, first_ref, second_ref, *refs):
    out_refs, held = refs[:-1], refs[-1]
    stacked = jnp.concatenate([first_ref[0], second_ref[0]], axis=0)
    held[...] = stacked.T.astype(jnp.float32)
    for k in range(X):
        first = lax.rem(place_ref[0] + k, X) * PIECE
        for m in range(PIECE):
            rows = held[pl.ds(first + m, ROWS, stride=BLOCK), :]
            out_ref = out_refs[k] if len(out_refs) > 1 else out_refs[0].at[k]
            out_ref[0, m % 2, m // 2 * ROWS : (m // 2 + 1) * ROWS] = rows.astype(jnp.bfloat16)


def turn_amplitudes(swapped, place, apart):
    piece = (PIECE, 2, QUARTER // 2, LANES)
    if apart:
        shapes = [jax.ShapeDtypeStruct(piece, jnp.bfloat16)] * X
        specs = [pl.BlockSpec((1, 2, QUARTER // 2, LANES), lambda i, place: (i, 0, 0, 0))] * X
    else:
        shapes = jax.ShapeDtypeStruct((X,) + piece, jnp.bfloat16)
        specs = pl.BlockSpec((X, 1, 2, QUARTER // 2, LANES), lambda i, place: (0, i, 0, 0, 0))
    return pl.pallas_call(
        amplitude_kernel,
        grid_spec=pltpu.PrefetchScalarGridSpec(
            num_scalar_prefetch=1,
            grid=(PIECE,),
            in_specs=[
                pl.BlockSpec((1, PAIRS, NV), lambda i, place: (place[1] * PIECE + i, 0, 0)),
                pl.BlockSpec((1, PAIRS, NV), lambda i, place: (place[2] * PIECE + i, 0, 0)),
            ],
            out_specs=specs,
            scratch_shapes=[pltpu.VMEM((NV, LANES), jnp.float32)],
        ),
        out_shape=shapes,
        compiler_params=pltpu.CompilerParams(vmem_limit_bytes=16 * 2**20),
        cost_estimate=cost(0, 2 * PAIRS * NV * BLOCK),
    )(place, swapped, swapped)


def join_kernel(source_ref, first_ref, second_ref, out_ref, low_held, high_held):
    first, second = first_ref[:, 0].astype(jnp.float32), second_ref[:, 0].astype(jnp.float32)
    low = lax.broadcasted_iota(jnp.int32, first.shape, 2) < PR
    low_held[...] = jnp.where(low, first, pltpu.roll(second, PR, 2)).reshape(ROWS * MESSAGE, LANES)
    high_held[...] = jnp.where(low, pltpu.roll(first, PR, 2), second).reshape(ROWS * MESSAGE, LANES)
    for e in range(PIECE):
        for side, held in enumerate((low_held, high_held)):
            for half in range(HALF):
                rows = held[pl.ds(half * PIECE + e, ROWS, stride=MESSAGE), :]
                out_ref[e, side, half * ROWS : (half + 1) * ROWS] = rows.astype(jnp.bfloat16)


def join_panels(got, sources):
    return pl.pallas_call(
        join_kernel,
        grid_spec=pltpu.PrefetchScalarGridSpec(
            num_scalar_prefetch=1,
            grid=(1,),
            in_specs=[
                pl.BlockSpec((ROWS, 1, MESSAGE, LANES), lambda i, source: (0, source[0], 0, 0)),
                pl.BlockSpec((ROWS, 1, MESSAGE, LANES), lambda i, source: (0, source[1], 0, 0)),
            ],
            out_specs=pl.BlockSpec((PIECE, 2, QUARTER // 2, LANES), lambda i, source: (0, 0, 0, 0)),
            scratch_shapes=[pltpu.VMEM((ROWS * MESSAGE, LANES), jnp.float32)] * 2,
        ),
        out_shape=jax.ShapeDtypeStruct((PIECE, 2, QUARTER // 2, LANES), jnp.bfloat16),
        compiler_params=pltpu.CompilerParams(vmem_limit_bytes=16 * 2**20),
        cost_estimate=cost(0, 3 * DEPTH * LANES * 2),
    )(sources, got, got)


def contract_kernel(*refs):
    left, (own_ref, other_ref), out_refs = refs[: 2 * X], refs[2 * X : 2 * X + 2], refs[2 * X + 2 :]
    both = jnp.concatenate([own_ref[...], other_ref[...]], axis=1)
    for k in range(2 * X):
        total = lax.dot_general(left[k][...], both, (((0,), (0,)), ((), ())), preferred_element_type=jnp.float32)
        side = lax.rem(k + lax.axis_index("zb"), 2)
        out_refs[k // 2][side] = total[:PAIRS, :LANES] + total[PAIRS:, LANES:]


def contract(left, right):
    left = [part.reshape(DEPTH, LANES) for part in left]
    right = [part.reshape(DEPTH, LANES) for part in right]
    return pl.pallas_call(
        contract_kernel,
        in_specs=[pl.BlockSpec(memory_space=pltpu.VMEM)] * (2 * X + 2),
        out_specs=[pl.BlockSpec(memory_space=pltpu.VMEM)] * X,
        out_shape=[jax.ShapeDtypeStruct((2, PAIRS, LANES), jnp.float32)] * X,
        compiler_params=pltpu.CompilerParams(vmem_limit_bytes=32 * 2**20),
        cost_estimate=cost(2 * 1024 * 1600 * 256, 5 * 2**20),
    )(*left, *right)


def shift_x(array, k):
    return lax.ppermute(array, "x", [(x, (x + k) % X) for x in range(X)])


def swap_zl(array, bit):
    return lax.ppermute(array, Z, [(z, z ^ bit) for z in range(ZL)])


def over_x(integrals, owners, offsets):
    pieces = slice_panel((1, 2, 3), integrals, owners, offsets)
    got = [shift_x(pieces[k - 1], k) for k in range(1, X)]
    owners, _ = lax.optimization_barrier((owners, pieces[0]))
    return list(slice_panel((0,), integrals, owners, offsets)) + got


def local(amplitudes, integrals, owners, offsets):
    got = over_x(integrals, owners, offsets)

    x, zl = lax.axis_index("x"), lax.axis_index(Z)
    owner_x, owner_z = lax.shift_right_logical(owners, 2), lax.bitwise_and(owners, 3)
    same_owner = owners[0] == owners[1]
    same_z = owner_z[0] == owner_z[1]
    at_z = [owner_z[0], jnp.where(same_z, lax.bitwise_xor(owner_z[1], 1), owner_z[1])]
    distance = lax.bitwise_and(x - owner_x, 3)
    choice = jnp.where(zl == at_z[1], jnp.where(same_z, X, distance[1]), distance[0])

    swapped = jnp.transpose(amplitudes, (2, 0, 1))
    places = [jnp.stack([x, lax.bitwise_xor(zl, k), lax.bitwise_xor(zl, k + 2)]).astype(jnp.int32) for k in range(2)]
    others = swap_zl(turn_amplitudes(swapped, places[1], False), 1)
    owns = turn_amplitudes(swapped, places[0], True)
    got, owns = lax.optimization_barrier((got, owns))

    def stay(*operands):
        return pl.pallas_call(
            lambda out_ref: None,
            out_specs=pl.BlockSpec(memory_space=pl.ANY),
            out_shape=jax.ShapeDtypeStruct((PIECE, PR, NV), jnp.bfloat16),
        )()

    def move(place, owners, offsets, integrals, *got):
        return swap_zl(lax.select_n(place, *got), 1)

    def again(place, owners, offsets, integrals, *got):
        got = over_x(integrals, owners, jnp.stack([offsets[1], offsets[1]]))
        return swap_zl(lax.select_n(place, *got), 1)

    case = jnp.where(same_owner, 2, jnp.where(same_z, 1, 0))
    moved = lax.switch(case, [stay, move, again], distance[1], owners, offsets, integrals, *got)

    left = [owns[0], others[0]]
    for k in range(1, X):
        left += [shift_x(owns[k], k), shift_x(others[k], k)]

    message = turn_panel(choice, got + [moved])
    spread = lax.all_to_all(message, ROW + Z, 0, 0, tiled=True)
    mine = join_panels(spread.reshape(ROWS, ZL, MESSAGE, LANES), jnp.stack(at_z).astype(jnp.int32))
    part = contract(left, [mine, swap_zl(mine, 2)])

    total = part[0]
    for k in range(1, X):
        total = total + shift_x(part[k], -k)
    spread = lax.all_to_all(total.reshape(2 * ROWS, PAIRS // ROWS, LANES), ("zb",) + ROW, 0, 0, tiled=True)
    return jnp.sum(spread, axis=0)


def solution(mesh):
    fine = Mesh(mesh.devices.reshape(2, 4, 2, X, 2, 2), ROW + COL)
    in_specs = (P(COL, None, ROW), P(COL, ROW, None), P(), P())
    out_specs = P(COL + ROW, None)
    return jax.shard_map(local, mesh=fine, in_specs=in_specs, out_specs=out_specs, check_vma=False)
```

```python
import functools

import jax
import jax.numpy as jnp
from jax import lax
from jax.experimental import pallas as pl
from jax.experimental.pallas import tpu as pltpu
from jax.sharding import Mesh
from jax.sharding import PartitionSpec as P

PR = 64
STEPS = 2
X = 4
ZL = 4
ROW = ("zh", "y", "core")
Z = ("za", "zb")
COL = ("x",) + Z
ROWS = 16
NV = 640
BLOCK = 40
PIECE = 10
HALF = PIECE // 2
PAIRS = 64
LANES = 128
QUARTER = NV // X
DEPTH = PIECE * QUARTER
CHUNK = 16
MESSAGE = 56


def cost(flops, moved):
    return pl.CostEstimate(flops=flops, bytes_accessed=moved, transcendentals=0)


def slice_kernel(steps, owners_ref, offsets_ref, integrals_ref, *refs):
    out_refs, (held, rows, sems) = refs[: len(steps)], refs[len(steps) :]
    i = pl.program_id(0)
    x = lax.axis_index("x")
    owns_second = jnp.logical_and(x * ZL + 2 * lax.axis_index("za") + lax.axis_index("zb") == owners_ref[1], owners_ref[0] != owners_ref[1])
    start = jnp.where(owns_second, offsets_ref[1], offsets_ref[0])

    def copy(chunk):
        source = integrals_ref.at[pl.ds(start + chunk * CHUNK, CHUNK)]
        return pltpu.make_async_copy(source, held.at[chunk], sems.at[chunk])

    @pl.when(i == 0)
    def _():
        for chunk in range(PR // CHUNK):
            copy(chunk).start()

    for chunk in range(PR // CHUNK):

        @pl.when(i == chunk)
        def _():
            copy(chunk).wait()

    for t in range(NV // LANES):
        lanes = slice(t * LANES, (t + 1) * LANES)
        rows[...] = held[i, :, :, lanes].astype(jnp.float32).reshape(CHUNK * BLOCK, LANES)
        for out_ref, k in zip(out_refs, steps):
            first = lax.rem(x + k, X) * PIECE
            for m in range(PIECE):
                out_ref[m, :, lanes] = rows[pl.ds(first + m, CHUNK, stride=BLOCK), :].astype(jnp.bfloat16)


def slice_panel(steps, integrals, owners, offsets):
    piece = jax.ShapeDtypeStruct((PIECE, PR, NV), jnp.bfloat16)
    return pl.pallas_call(
        functools.partial(slice_kernel, steps),
        grid_spec=pltpu.PrefetchScalarGridSpec(
            num_scalar_prefetch=2,
            grid=(PR // CHUNK,),
            in_specs=[pl.BlockSpec(memory_space=pl.ANY)],
            out_specs=[pl.BlockSpec((PIECE, CHUNK, NV), lambda i, owners, offsets: (0, i, 0))] * len(steps),
            scratch_shapes=[
                pltpu.VMEM((PR // CHUNK, CHUNK, BLOCK, NV), jnp.bfloat16),
                pltpu.VMEM((CHUNK * BLOCK, LANES), jnp.float32),
                pltpu.SemaphoreType.DMA((PR // CHUNK,)),
            ],
        ),
        out_shape=[piece] * len(steps),
        compiler_params=pltpu.CompilerParams(vmem_limit_bytes=24 * 2**20),
        cost_estimate=cost(0, 4 * PR * BLOCK * NV),
    )(owners, offsets, integrals)


def turn_kernel(choice_ref, *refs):
    piece_refs, out_ref, (held, turned, message, sems) = refs[: X + 1], refs[X + 1], refs[X + 2 :]
    for k in range(X + 1):

        @pl.when(choice_ref[0] == k)
        def _():
            for half in range(HALF):
                pltpu.make_async_copy(piece_refs[k].at[half], held.at[half], sems.at[half]).start()

    for row in range(PIECE * HALF, MESSAGE):
        message[pl.ds(row, ROWS * ZL, stride=MESSAGE), :] = jnp.zeros((ROWS * ZL, LANES), jnp.float32)
    for half in range(HALF):
        pltpu.make_async_copy(piece_refs[0].at[half], held.at[half], sems.at[half]).wait()
        turned[half * NV : (half + 1) * NV, :] = held[half].T.astype(jnp.float32)
    for half in range(HALF):
        for e in range(PIECE):
            rows = turned[pl.ds(half * NV + e, ROWS * ZL, stride=PIECE), :]
            message[pl.ds(half * PIECE + e, ROWS * ZL, stride=MESSAGE), :] = rows
    out_ref[...] = message[...].astype(jnp.bfloat16).reshape(ROWS * ZL, MESSAGE, LANES)


def turn_panel(choice, pieces):
    pieces = [piece.reshape(HALF, LANES, NV) for piece in pieces]
    return pl.pallas_call(
        turn_kernel,
        grid_spec=pltpu.PrefetchScalarGridSpec(
            num_scalar_prefetch=1,
            grid=(1,),
            in_specs=[pl.BlockSpec(memory_space=pl.ANY)] * (X + 1),
            out_specs=pl.BlockSpec((ROWS * ZL, MESSAGE, LANES), lambda i, choice: (0, 0, 0)),
            scratch_shapes=[
                pltpu.VMEM((HALF, LANES, NV), jnp.bfloat16),
                pltpu.VMEM((HALF * NV, LANES), jnp.float32),
                pltpu.VMEM((ROWS * ZL * MESSAGE, LANES), jnp.float32),
                pltpu.SemaphoreType.DMA((HALF,)),
            ],
        ),
        out_shape=jax.ShapeDtypeStruct((ROWS * ZL, MESSAGE, LANES), jnp.bfloat16),
        compiler_params=pltpu.CompilerParams(vmem_limit_bytes=24 * 2**20),
        cost_estimate=cost(0, 4 * LANES * NV * HALF),
    )(choice[None].astype(jnp.int32), *pieces)


def amplitude_kernel(place_ref, first_ref, second_ref, *refs):
    out_refs, held = refs[:-1], refs[-1]
    stacked = jnp.concatenate([first_ref[0], second_ref[0]], axis=0)
    held[...] = stacked.T.astype(jnp.float32)
    for k in range(X):
        first = lax.rem(place_ref[0] + k, X) * PIECE
        for m in range(PIECE):
            rows = held[pl.ds(first + m, ROWS, stride=BLOCK), :]
            out_ref = out_refs[k] if len(out_refs) > 1 else out_refs[0].at[k]
            out_ref[0, m % 2, m // 2 * ROWS : (m // 2 + 1) * ROWS] = rows.astype(jnp.bfloat16)


def turn_amplitudes(swapped, place, apart):
    piece = (PIECE, 2, QUARTER // 2, LANES)
    if apart:
        shapes = [jax.ShapeDtypeStruct(piece, jnp.bfloat16)] * X
        specs = [pl.BlockSpec((1, 2, QUARTER // 2, LANES), lambda i, place: (i, 0, 0, 0))] * X
    else:
        shapes = jax.ShapeDtypeStruct((X,) + piece, jnp.bfloat16)
        specs = pl.BlockSpec((X, 1, 2, QUARTER // 2, LANES), lambda i, place: (0, i, 0, 0, 0))
    return pl.pallas_call(
        amplitude_kernel,
        grid_spec=pltpu.PrefetchScalarGridSpec(
            num_scalar_prefetch=1,
            grid=(PIECE,),
            in_specs=[
                pl.BlockSpec((1, PAIRS, NV), lambda i, place: (place[1] * PIECE + i, 0, 0)),
                pl.BlockSpec((1, PAIRS, NV), lambda i, place: (place[2] * PIECE + i, 0, 0)),
            ],
            out_specs=specs,
            scratch_shapes=[pltpu.VMEM((NV, LANES), jnp.float32)],
        ),
        out_shape=shapes,
        compiler_params=pltpu.CompilerParams(vmem_limit_bytes=16 * 2**20),
        cost_estimate=cost(0, 2 * PAIRS * NV * BLOCK),
    )(place, swapped, swapped)


def join_kernel(source_ref, first_ref, second_ref, out_ref, low_held, high_held):
    first, second = first_ref[:, 0].astype(jnp.float32), second_ref[:, 0].astype(jnp.float32)
    low = lax.broadcasted_iota(jnp.int32, first.shape, 2) < PR
    low_held[...] = jnp.where(low, first, pltpu.roll(second, PR, 2)).reshape(ROWS * MESSAGE, LANES)
    high_held[...] = jnp.where(low, pltpu.roll(first, PR, 2), second).reshape(ROWS * MESSAGE, LANES)
    for e in range(PIECE):
        for side, held in enumerate((low_held, high_held)):
            for half in range(HALF):
                rows = held[pl.ds(half * PIECE + e, ROWS, stride=MESSAGE), :]
                out_ref[e, side, half * ROWS : (half + 1) * ROWS] = rows.astype(jnp.bfloat16)


def join_panels(got, sources):
    return pl.pallas_call(
        join_kernel,
        grid_spec=pltpu.PrefetchScalarGridSpec(
            num_scalar_prefetch=1,
            grid=(1,),
            in_specs=[
                pl.BlockSpec((ROWS, 1, MESSAGE, LANES), lambda i, source: (0, source[0], 0, 0)),
                pl.BlockSpec((ROWS, 1, MESSAGE, LANES), lambda i, source: (0, source[1], 0, 0)),
            ],
            out_specs=pl.BlockSpec((PIECE, 2, QUARTER // 2, LANES), lambda i, source: (0, 0, 0, 0)),
            scratch_shapes=[pltpu.VMEM((ROWS * MESSAGE, LANES), jnp.float32)] * 2,
        ),
        out_shape=jax.ShapeDtypeStruct((PIECE, 2, QUARTER // 2, LANES), jnp.bfloat16),
        compiler_params=pltpu.CompilerParams(vmem_limit_bytes=16 * 2**20),
        cost_estimate=cost(0, 3 * DEPTH * LANES * 2),
    )(sources, got, got)


def contract_kernel(*refs):
    left, (own_ref, other_ref), out_refs = refs[: 2 * X], refs[2 * X : 2 * X + 2], refs[2 * X + 2 :]
    both = jnp.concatenate([own_ref[...], other_ref[...]], axis=1)
    for k in range(2 * X):
        total = lax.dot_general(left[k][...], both, (((0,), (0,)), ((), ())), preferred_element_type=jnp.float32)
        side = lax.rem(k + lax.axis_index("zb"), 2)
        out_refs[k // 2][side] = total[:PAIRS, :LANES] + total[PAIRS:, LANES:]


def contract(left, right):
    left = [part.reshape(DEPTH, LANES) for part in left]
    right = [part.reshape(DEPTH, LANES) for part in right]
    return pl.pallas_call(
        contract_kernel,
        in_specs=[pl.BlockSpec(memory_space=pltpu.VMEM)] * (2 * X + 2),
        out_specs=[pl.BlockSpec(memory_space=pltpu.VMEM)] * X,
        out_shape=[jax.ShapeDtypeStruct((2, PAIRS, LANES), jnp.float32)] * X,
        compiler_params=pltpu.CompilerParams(vmem_limit_bytes=32 * 2**20),
        cost_estimate=cost(2 * 1024 * 1600 * 256, 5 * 2**20),
    )(*left, *right)


def shift_x(array, k):
    return lax.ppermute(array, "x", [(x, (x + k) % X) for x in range(X)])


def swap_zl(array, bit):
    return lax.ppermute(array, Z, [(z, z ^ bit) for z in range(ZL)])


def over_x(integrals, owners, offsets):
    pieces = slice_panel((1, 2, 3), integrals, owners, offsets)
    got = [shift_x(pieces[k - 1], k) for k in range(1, X)]
    owners, _ = lax.optimization_barrier((owners, pieces[0]))
    return list(slice_panel((0,), integrals, owners, offsets)) + got


def local(amplitudes, integrals, owners, offsets):
    got = over_x(integrals, owners, offsets)

    x, zl = lax.axis_index("x"), lax.axis_index(Z)
    owner_x, owner_z = lax.shift_right_logical(owners, 2), lax.bitwise_and(owners, 3)
    same_owner = owners[0] == owners[1]
    same_z = owner_z[0] == owner_z[1]
    at_z = [owner_z[0], jnp.where(same_z, lax.bitwise_xor(owner_z[1], 1), owner_z[1])]
    distance = lax.bitwise_and(x - owner_x, 3)
    choice = jnp.where(zl == at_z[1], jnp.where(same_z, X, distance[1]), distance[0])

    swapped = jnp.transpose(amplitudes, (2, 0, 1))
    places = [jnp.stack([x, lax.bitwise_xor(zl, k), lax.bitwise_xor(zl, k + 2)]).astype(jnp.int32) for k in range(2)]
    others = swap_zl(turn_amplitudes(swapped, places[1], False), 1)
    owns = turn_amplitudes(swapped, places[0], True)
    got, owns = lax.optimization_barrier((got, owns))

    def stay(*operands):
        return pl.pallas_call(
            lambda out_ref: None,
            out_specs=pl.BlockSpec(memory_space=pl.ANY),
            out_shape=jax.ShapeDtypeStruct((PIECE, PR, NV), jnp.bfloat16),
        )()

    def move(place, owners, offsets, integrals, *got):
        return swap_zl(lax.select_n(place, *got), 1)

    def again(place, owners, offsets, integrals, *got):
        got = over_x(integrals, owners, jnp.stack([offsets[1], offsets[1]]))
        return swap_zl(lax.select_n(place, *got), 1)

    case = jnp.where(same_owner, 2, jnp.where(same_z, 1, 0))
    moved = lax.switch(case, [stay, move, again], distance[1], owners, offsets, integrals, *got)

    left = [owns[0], others[0]]
    for k in range(1, X):
        left += [shift_x(owns[k], k), shift_x(others[k], k)]

    message = turn_panel(choice, got + [moved])
    spread = lax.all_to_all(message, ROW + Z, 0, 0, tiled=True)
    mine = join_panels(spread.reshape(ROWS, ZL, MESSAGE, LANES), jnp.stack(at_z).astype(jnp.int32))
    part = contract(left, [mine, swap_zl(mine, 2)])

    total = part[0]
    for k in range(1, X):
        total = total + shift_x(part[k], -k)
    spread = lax.all_to_all(total.reshape(2 * ROWS, PAIRS // ROWS, LANES), ("zb",) + ROW, 0, 0, tiled=True)
    return jnp.sum(spread, axis=0)


def solution(mesh):
    fine = Mesh(mesh.devices.reshape(2, 4, 2, X, 2, 2), ROW + COL)
    in_specs = (P(COL, None, ROW), P(COL, ROW, None), P(), P())
    out_specs = P(COL + ROW, None)
    return jax.shard_map(local, mesh=fine, in_specs=in_specs, out_specs=out_specs, check_vma=False)
```
